32 devices in a mesh: ctx: 8 (over z, y), head: 4 (over x, core).
Axes of the slice: x: 2, y: 2, z: 4, core: 2. Of those that a mesh axis runs over, the one named last changes fastest.
Arguments:
- queries: bfloat16 [4, 2048, 1024], P('head', 'ctx'), may hold values from -6 to 6
- keys: bfloat16 [4, 2048, 128], P('head', 'ctx'), may hold values from -6 to 6
- values: bfloat16 [4, 2048, 128], P('head', 'ctx'), may hold values from -6 to 6
- documents: int32 [4, 2048], P('head', 'ctx'), may hold values from 0 to 3, never falling along the last dimension, each value on 1 to 1024 neighbouring positions
Outputs:
- tokens_out: bfloat16 [4, 2048, 1024], P(None, ('ctx', 'head'))
- log_sums: float32 [4, 8, 2048], P('head', None, 'ctx')
The draws below stay inside these ranges and needn't reach their ends.
Inputs may be any that keep to these rules, and one draw needn't show every extreme that they name: `documents`: each row's ids never fall along positions; each document holds at most half of the 2048 positions.
All inputs are finite; a program needn't handle non-finite values.
Results may differ from the reference program's by a relative error of at most 0.0075.
Values may be sent and summed in bfloat16 or wider, within the bound.
A program may use at most 64 MiB of HBM per device.

```python
import math
import jax
import jax.numpy as jnp
import numpy as np
from jax import lax

HD = 128
G = 8
SPAN = 256
DOCS = 4
UNITS = 4
L = 2048


def draw_queries(key, part):
    own_key = jax.random.fold_in(key, 1)
    array_shape = (UNITS, L, G * HD)
    return jax.random.truncated_normal(own_key, -6.0, 6.0, array_shape, jnp.float32).astype(jnp.bfloat16)


def draw_keys(key, part):
    own_key = jax.random.fold_in(key, 2)
    array_shape = (UNITS, L, HD)
    return jax.random.truncated_normal(own_key, -6.0, 6.0, array_shape, jnp.float32).astype(jnp.bfloat16)


def levels(key, extent, cuts, low, high):
    def one(axis_at, shards_of):
        heights = jax.random.uniform(jax.random.fold_in(jax.random.fold_in(key, 6), axis_at), (shards_of,), jnp.float32, low / len(cuts), high / len(cuts))
        return jnp.repeat(jnp.exp(heights), extent[axis_at] // shards_of).reshape((-1,) + (1,) * (len(extent) - axis_at - 1))

    gain = one(*cuts[0])
    for cut in cuts[1:]:
        gain = gain * one(*cut)
    return gain


def split_up(amount, total, limit, lean):
    weights = [(1 << 20) // math.isqrt(rank ** lean) + 1 for rank in range(2, amount + 1)]
    spare, given = total - limit - (amount - 1), [1] * (amount - 1)
    while spare > 0:
        movable = [i for i in range(amount - 1) if given[i] < limit]
        pool, left = sum([weights[i] for i in movable]), spare
        for i in movable:
            more = min(limit - given[i], max(1, left * weights[i] // pool), spare)
            given[i] = given[i] + more
            spare = spare - more
    return np.array([limit] + given)


def uneven_parts(key, count, total, limit, slope):
    if count == 2:
        one = jax.random.randint(key, (), max(1, total - limit), min(limit, total - 1) + 1)
        return jnp.stack([one, total - one])
    sizes = jnp.asarray(split_up(count, total, limit, slope), jnp.int32)
    twos = (count - 1) // 2
    donor, receiver = sizes[1:1 + 2 * twos:2], sizes[2:2 + 2 * twos:2]
    room = jnp.minimum(donor - 1, limit - receiver)
    moved = jax.random.randint(jax.random.fold_in(key, 1), (twos,), 0, 1 << 20) % (room + 1)
    sizes = sizes.at[1:1 + 2 * twos:2].set(donor - moved).at[2:2 + 2 * twos:2].set(receiver + moved)
    return sizes[jax.random.permutation(jax.random.fold_in(key, 2), count)]


def gaussian(key, shape, spread, bound, pieces=(), kind=jnp.bfloat16):
    loudness = levels(key, shape, pieces, -0.22, 0.18) if pieces else 1.0
    result = jax.random.normal(key, shape, jnp.float32) * spread * loudness
    return jnp.minimum(jnp.maximum(result, -bound), bound).astype(kind)


def setup_inputs(seed: int = 0) -> dict:
    key_list = jax.random.split(jax.random.key(seed), 5)
    return {
        "queries": draw_queries(jax.random.fold_in(key_list[4], 71), 0),
        "keys": draw_keys(jax.random.fold_in(key_list[4], 71), 0),
        "values": gaussian(key_list[2], (UNITS, L, HD), 1.0, 6.0, ((0, 4), (1, 8))),
        "documents": jax.vmap(lambda own: jnp.searchsorted(jnp.cumsum(uneven_parts(own, DOCS, L, L // 2, 2)), jnp.arange(L), side="right"))(jax.random.split(key_list[3], UNITS)).reshape((UNITS, L)).astype(jnp.int32),
    }


def reference(queries, keys, values, documents):
    score_scale = 1.0 / (HD ** 0.5)
    positions = jnp.arange(L, dtype=jnp.int32)

    def one_unit(unit_data):
        unit_q, unit_k, unit_v, unit_doc = unit_data
        key_f = unit_k.astype(jnp.float32)
        value_f = unit_v.astype(jnp.float32)
        blocked_q = unit_q.reshape(L // SPAN, SPAN, G, HD)
        blocked_pos = positions.reshape(L // SPAN, SPAN)
        blocked_doc = unit_doc.reshape(L // SPAN, SPAN)

        def one_block(query_block):
            query_rows, query_pos, query_doc = query_block
            scores = jnp.einsum("qgd,kd->gqk", query_rows.astype(jnp.float32), key_f) * score_scale
            visible = (positions[None, :] <= query_pos[:, None]) & (unit_doc[None, :] == query_doc[:, None])
            scores = jnp.where(visible[None], scores, -jnp.inf)
            row_max = jnp.max(scores, axis=2)
            weights = jnp.where(visible[None], jnp.exp(scores - row_max[:, :, None]), 0.0)
            row_total = jnp.sum(weights, axis=2)
            rounded = lax.optimization_barrier(weights.astype(jnp.bfloat16))
            mixed_rows = jnp.einsum("gqk,kd->qgd", rounded.astype(jnp.float32), value_f)
            normed = (mixed_rows / jnp.transpose(row_total)[:, :, None]).astype(jnp.bfloat16)
            return normed.reshape(SPAN, G * HD), row_max + jnp.log(row_total)

        unit_outs, unit_lse = lax.map(one_block, (blocked_q, blocked_pos, blocked_doc))
        return unit_outs.reshape(L, G * HD), jnp.transpose(unit_lse, (1, 0, 2)).reshape(G, L)

    tokens_out, log_sums = lax.map(one_unit, (queries, keys, values, documents))
    return tokens_out, log_sums
```

```python
import functools
import math

import jax
import jax.numpy as jnp
from jax import lax
from jax.experimental import pallas as pl
from jax.experimental.pallas import tpu as pltpu
from jax.sharding import PartitionSpec as P

MASKED = -1e30
LANES = 128
MESH = pl.DeviceIdType.MESH


def flip(index, mask):
    out = index
    bit = 1
    while bit <= mask:
        if mask & bit:
            out = out + bit * (1 - 2 * (lax.rem(lax.div(index, bit), 2)))
        bit *= 2
    return out


def kernel(
    n_ctx,
    n_head,
    q_hbm,
    k_hbm,
    v_hbm,
    doc_ref,
    out_ref,
    lse_ref,
    q_in,
    q_rows,
    row_doc,
    row_at,
    own_k,
    own_v,
    z_k,
    z_v,
    y_k,
    y_v,
    run_max,
    run_sum,
    run_acc,
    stage,
    lse_cols,
    in_sem,
    z_send,
    z_recv,
    y_send,
    y_recv,
    o_send,
    o_recv,
):
    span = own_v.shape[0]
    head_dim = own_v.shape[1]
    groups = q_in.shape[1] // head_dim
    piece = span // n_head
    pairs, hops = n_ctx // 2, n_ctx // 4
    scale = math.log2(math.e) / math.sqrt(head_dim)

    me = lax.axis_index("ctx")
    head = lax.axis_index("head")
    pair, side = lax.div(me, 2), lax.rem(me, 2)
    partner = me + 1 - 2 * side
    up = lax.rem(me + 2, n_ctx)
    down = lax.rem(me + n_ctx - 2, n_ctx)

    loads = [
        pltpu.make_async_copy(k_hbm, own_k.at[pl.ds(0, span)], in_sem.at[0]),
        pltpu.make_async_copy(v_hbm, own_v, in_sem.at[1]),
        pltpu.make_async_copy(q_hbm, q_in, in_sem.at[2]),
    ]
    for load in loads:
        load.start()
    barrier = pltpu.get_barrier_semaphore()
    for other in (up, down, partner):
        pl.semaphore_signal(barrier, inc=1, device_id={"ctx": other}, device_id_type=MESH)
    for mask in range(1, n_head):
        pl.semaphore_signal(
            barrier, inc=1, device_id={"head": flip(head, mask)}, device_id_type=MESH
        )

    docs = doc_ref[...].astype(jnp.float32)
    tail = own_k.shape[0] - span
    doc_tile = jnp.concatenate(
        [docs[:, at : at + LANES] for at in range(0, span, LANES)]
        + [jnp.zeros((tail - span // LANES, LANES), jnp.float32)],
        axis=0,
    )
    own_k[pl.ds(span, tail), :] = doc_tile.astype(jnp.bfloat16)
    loads[0].wait()
    loads[1].wait()
    pl.semaphore_wait(barrier, 3 + n_head - 1)

    def z_copy(hop, part):
        if part == 0:
            source = own_k if hop == 1 else z_k.at[hop - 2]
            target = z_k.at[hop - 1]
        else:
            source = own_v if hop == 1 else z_v.at[hop - 2]
            target = z_v.at[hop - 1]
        return pltpu.make_async_remote_copy(
            src_ref=source,
            dst_ref=target,
            send_sem=z_send.at[hop - 1, part],
            recv_sem=z_recv.at[hop - 1, part],
            device_id={"ctx": up},
            device_id_type=MESH,
        )

    def y_copy(held, hop, part):
        if part == 0:
            source = own_k if held == 0 else z_k.at[held - 1]
            target = y_k.at[hop - 1]
        else:
            source = own_v if held == 0 else z_v.at[held - 1]
            target = y_v.at[hop - 1]
        return pltpu.make_async_remote_copy(
            src_ref=source,
            dst_ref=target,
            send_sem=y_send.at[hop - 1, part],
            recv_sem=y_recv.at[hop - 1, part],
            device_id={"ctx": partner},
            device_id_type=MESH,
        )

    has_up = pair + 1 < pairs

    def sends(held, part, act):
        if held < hops:

            @pl.when(has_up & (pair >= held))
            def _():
                act(z_copy(held + 1, part))

            @pl.when((side == 0) & (pair >= held))
            def _():
                act(y_copy(held, held + 1, part))

        if held > 0:

            @pl.when((side == 1) & (pair >= held))
            def _():
                act(y_copy(held, held, part))

    for part in range(2):
        sends(0, part, lambda copy: copy.start())

    doc_cols = jnp.transpose(jnp.broadcast_to(docs, (LANES, span)))
    lse_cols[...] = doc_cols
    loads[2].wait()
    for turn in range(n_head):
        dest = flip(head, n_head - 1 - turn)
        rows = pl.ds(pl.multiple_of(dest * piece, piece), piece)
        for group in range(groups):
            q_rows[turn, pl.ds(group * piece, piece), :] = q_in[
                rows, pl.ds(group * head_dim, head_dim)
            ]
        row_doc[turn] = lse_cols[rows, :]
        row_at[turn] = dest * piece + lax.broadcasted_iota(jnp.int32, (piece, LANES), 0)

    def attend(turn, k_ref, v_ref, diagonal):
        key_docs = k_ref[pl.ds(span, tail), :].astype(jnp.float32)
        biases = []
        for at in range(span // LANES):
            seen = row_doc[turn] == key_docs[at : at + 1, :]
            if diagonal:
                key_at = at * LANES + lax.broadcasted_iota(jnp.int32, (piece, LANES), 1)
                seen = seen & (key_at <= row_at[turn])
            biases.append(jnp.where(seen, 0.0, MASKED))
        bias = jnp.concatenate(biases, axis=1)
        scores = lax.dot_general(
            q_rows[turn],
            k_ref[pl.ds(0, span), :],
            (((1,), (1,)), ((), ())),
            preferred_element_type=jnp.float32,
        )
        scores = scores * scale + jnp.concatenate([bias] * groups, axis=0)
        top = jnp.max(scores, axis=1, keepdims=True)
        top = jnp.broadcast_to(top, (groups * piece, LANES))
        if not diagonal:
            old = run_max[turn]
            top = jnp.maximum(top, old)
        weights = [
            jnp.exp2(scores[:, at : at + LANES] - top) for at in range(0, span, LANES)
        ]
        total = functools.reduce(jnp.add, weights)
        mixed = jnp.dot(
            jnp.concatenate([w.astype(jnp.bfloat16) for w in weights], axis=1),
            v_ref[...],
            preferred_element_type=jnp.float32,
        )
        run_max[turn] = top
        if diagonal:
            run_sum[turn] = total
            run_acc[turn] = mixed
        else:
            factor = jnp.exp2(old - top)
            run_sum[turn] = run_sum[turn] * factor + total
            run_acc[turn] = run_acc[turn] * factor + mixed

    def attend_all(k_ref, v_ref, diagonal=False):
        def step(turn, carry):
            attend(turn, k_ref, v_ref, diagonal)
            return carry

        lax.fori_loop(0, n_head, step, 0, unroll=min(4, n_head))

    attend_all(own_k, own_v, True)

    def y_there(hop):
        return pair + side >= hop

    for hop in range(1, hops + 1):

        @pl.when(pair >= hop)
        def _():
            z_copy(hop, 0).wait_recv()

        sends(hop, 0, lambda copy: copy.start())
        if hop > 1:

            @pl.when(y_there(hop - 1))
            def _():
                for part in range(2):
                    y_copy(0, hop - 1, part).wait_recv()
                attend_all(y_k.at[hop - 2], y_v.at[hop - 2])

        @pl.when(pair >= hop)
        def _():
            z_copy(hop, 1).wait_recv()

        sends(hop, 1, lambda copy: copy.start())

        @pl.when(pair >= hop)
        def _():
            attend_all(z_k.at[hop - 1], z_v.at[hop - 1])

    @pl.when(y_there(hops))
    def _():
        for part in range(2):
            y_copy(0, hops, part).wait_recv()

    def out_copy(turn, slot):
        return pltpu.make_async_remote_copy(
            src_ref=stage.at[turn],
            dst_ref=out_ref.at[slot],
            send_sem=o_send.at[turn],
            recv_sem=o_recv.at[turn],
            device_id={"head": flip(head, n_head - 1 - turn)},
            device_id_type=MESH,
        )

    lane = lax.broadcasted_iota(jnp.int32, (piece, LANES), 1)
    for turn in range(n_head):

        @pl.when(y_there(hops))
        def _():
            attend(turn, y_k.at[hops - 1], y_v.at[hops - 1], False)

        dest = flip(head, n_head - 1 - turn)
        total = jnp.sum(run_sum[turn], axis=1, keepdims=True)
        total = jnp.broadcast_to(total, (groups * piece, LANES))
        normed = (run_acc[turn] * (1.0 / total)).astype(jnp.bfloat16)
        for group in range(groups):
            block = normed[group * piece : (group + 1) * piece]
            columns = pl.ds(group * head_dim, head_dim)
            if turn < n_head - 1:
                stage[turn, :, columns] = block
            else:
                out_ref[head, :, columns] = block
        if turn < n_head - 1:
            out_copy(turn, head).start()
        log_sum = run_max[turn] * math.log(2.0) + jnp.log(total)
        columns = jnp.zeros((piece, LANES), jnp.float32)
        for group in range(groups):
            columns = jnp.where(
                lane == group, log_sum[group * piece : (group + 1) * piece], columns
            )
        lse_cols[pl.ds(pl.multiple_of(dest * piece, piece), piece), :] = columns

    lse_ref[...] = jnp.transpose(lse_cols[...])[:groups]

    for held in range(hops + 1):
        for part in range(2):
            sends(held, part, lambda copy: copy.wait_send())
    for turn in range(n_head - 1):
        out_copy(turn, head).wait_send()
    for turn in range(n_head - 1):
        out_copy(turn, flip(head, n_head - 1 - turn)).wait_recv()


def body(n_ctx, n_head, queries, keys, values, documents):
    span, width = queries.shape[1:]
    head_dim = keys.shape[2]
    groups = width // head_dim
    piece, hops, tail = span // n_head, n_ctx // 4, 16
    vmem = pl.BlockSpec(memory_space=pltpu.VMEM)
    hbm = pl.BlockSpec(memory_space=pl.ANY)
    bf16, f32 = jnp.bfloat16, jnp.float32
    stacked = (n_head, groups * piece, LANES)
    out, lse = pl.pallas_call(
        functools.partial(kernel, n_ctx, n_head),
        out_shape=(
            jax.ShapeDtypeStruct((n_head, piece, width), bf16),
            jax.ShapeDtypeStruct((groups, span), f32),
        ),
        in_specs=[hbm, hbm, hbm, vmem],
        out_specs=(vmem, vmem),
        scratch_shapes=[
            pltpu.VMEM((span, width), bf16),
            pltpu.VMEM((n_head, groups * piece, head_dim), bf16),
            pltpu.VMEM((n_head, piece, LANES), f32),
            pltpu.VMEM((n_head, piece, LANES), jnp.int32),
            pltpu.VMEM((span + tail, head_dim), bf16),
            pltpu.VMEM((span, head_dim), bf16),
            pltpu.VMEM((hops, span + tail, head_dim), bf16),
            pltpu.VMEM((hops, span, head_dim), bf16),
            pltpu.VMEM((hops, span + tail, head_dim), bf16),
            pltpu.VMEM((hops, span, head_dim), bf16),
            pltpu.VMEM(stacked, f32),
            pltpu.VMEM(stacked, f32),
            pltpu.VMEM(stacked, f32),
            pltpu.VMEM((n_head, piece, width), bf16),
            pltpu.VMEM((span, LANES), f32),
            pltpu.SemaphoreType.DMA((3,)),
            pltpu.SemaphoreType.DMA((hops, 2)),
            pltpu.SemaphoreType.DMA((hops, 2)),
            pltpu.SemaphoreType.DMA((hops, 2)),
            pltpu.SemaphoreType.DMA((hops, 2)),
            pltpu.SemaphoreType.DMA((n_head,)),
            pltpu.SemaphoreType.DMA((n_head,)),
        ],
        compiler_params=pltpu.CompilerParams(
            collective_id=0, has_side_effects=True, vmem_limit_bytes=40 * 1024 * 1024
        ),
        cost_estimate=pl.CostEstimate(
            flops=2 * 2 * span * width * span * (2 * hops + 1),
            bytes_accessed=4 * span * width,
            transcendentals=span * groups * span * (2 * hops + 1),
        ),
    )(queries[0], keys[0], values[0], documents)
    return out, lse[None]


def solution(mesh):
    n_ctx, n_head = mesh.shape["ctx"], mesh.shape["head"]
    in_specs = (
        P("head", "ctx", None),
        P("head", "ctx", None),
        P("head", "ctx", None),
        P("head", "ctx"),
    )
    out_specs = (P(None, ("ctx", "head"), None), P("head", None, "ctx"))
    return jax.shard_map(
        functools.partial(body, n_ctx, n_head),
        mesh=mesh,
        in_specs=in_specs,
        out_specs=out_specs,
        check_vma=False,
    )
```

```python
import functools
import math

import jax
import jax.numpy as jnp
from jax import lax
from jax.experimental import pallas as pl
from jax.experimental.pallas import tpu as pltpu
from jax.sharding import PartitionSpec as P

MASKED = -1e30
LANES = 128
VMEM_GRANT = 63 * 1024 * 1024
MESH = pl.DeviceIdType.MESH


def flip(index, mask):
    out = index
    bit = 1
    while bit <= mask:
        if mask & bit:
            out = out + bit * (1 - 2 * (lax.rem(lax.div(index, bit), 2)))
        bit *= 2
    return out


def kernel(
    n_ctx,
    n_head,
    q_hbm,
    k_hbm,
    v_hbm,
    doc_hbm,
    out_ref,
    lse_ref,
    doc_ref,
    q_in,
    q_rows,
    row_doc,
    row_at,
    own_k,
    own_v,
    z_k,
    z_v,
    y_k,
    y_v,
    run_max,
    run_sum,
    run_acc,
    stage,
    lse_cols,
    lse_rows,
    in_sem,
    z_send,
    z_recv,
    y_send,
    y_recv,
    o_send,
    o_recv,
):
    span = own_v.shape[0]
    head_dim = own_v.shape[1]
    groups = q_in.shape[1] // head_dim
    piece = span // n_head
    pairs, hops = n_ctx // 2, n_ctx // 4
    scale = math.log2(math.e) / math.sqrt(head_dim)

    me = lax.axis_index("ctx")
    head = lax.axis_index("head")
    pair, side = lax.div(me, 2), lax.rem(me, 2)
    partner = me + 1 - 2 * side
    up, down = me + 2, me - 2
    has_up, has_down = pair + 1 < pairs, pair > 0

    loads = [
        pltpu.make_async_copy(k_hbm, own_k.at[pl.ds(0, span)], in_sem.at[0]),
        pltpu.make_async_copy(v_hbm, own_v, in_sem.at[1]),
        pltpu.make_async_copy(doc_hbm, doc_ref, in_sem.at[2]),
        pltpu.make_async_copy(q_hbm, q_in, in_sem.at[3]),
    ]
    for load in loads:
        load.start()
    barrier = pltpu.get_barrier_semaphore()

    @pl.when(has_up)
    def _():
        pl.semaphore_signal(barrier, inc=1, device_id={"ctx": up}, device_id_type=MESH)

    @pl.when(has_down)
    def _():
        pl.semaphore_signal(barrier, inc=1, device_id={"ctx": down}, device_id_type=MESH)

    pl.semaphore_signal(barrier, inc=1, device_id={"ctx": partner}, device_id_type=MESH)
    for mask in range(1, n_head):
        pl.semaphore_signal(
            barrier, inc=1, device_id={"head": flip(head, mask)}, device_id_type=MESH
        )

    loads[2].wait()
    docs = doc_ref[...].astype(jnp.float32)
    tail = own_k.shape[0] - span
    doc_tile = jnp.concatenate(
        [docs[:, at : at + LANES] for at in range(0, span, LANES)]
        + [jnp.zeros((tail - span // LANES, LANES), jnp.float32)],
        axis=0,
    )
    own_k[pl.ds(span, tail), :] = doc_tile.astype(jnp.bfloat16)
    loads[0].wait()
    loads[1].wait()
    pl.semaphore_wait(barrier, n_head + has_up.astype(jnp.int32) + has_down.astype(jnp.int32))

    def z_copy(hop, part):
        if part == 0:
            source = own_k if hop == 1 else z_k.at[hop - 2]
            target = z_k.at[hop - 1]
        else:
            source = own_v if hop == 1 else z_v.at[hop - 2]
            target = z_v.at[hop - 1]
        return pltpu.make_async_remote_copy(
            src_ref=source,
            dst_ref=target,
            send_sem=z_send.at[hop - 1, part],
            recv_sem=z_recv.at[hop - 1, part],
            device_id={"ctx": up},
            device_id_type=MESH,
        )

    def y_copy(held, hop, part):
        if part == 0:
            source = own_k if held == 0 else z_k.at[held - 1]
            target = y_k.at[hop - 1]
        else:
            source = own_v if held == 0 else z_v.at[held - 1]
            target = y_v.at[hop - 1]
        return pltpu.make_async_remote_copy(
            src_ref=source,
            dst_ref=target,
            send_sem=y_send.at[hop - 1, part],
            recv_sem=y_recv.at[hop - 1, part],
            device_id={"ctx": partner},
            device_id_type=MESH,
        )

    def sends(held, part, act):
        if held < hops:

            @pl.when(has_up & (pair >= held))
            def _():
                act(z_copy(held + 1, part))

            @pl.when((side == 0) & (pair >= held))
            def _():
                act(y_copy(held, held + 1, part))

        if held > 0:

            @pl.when((side == 1) & (pair >= held))
            def _():
                act(y_copy(held, held, part))

    for part in range(2):
        sends(0, part, lambda copy: copy.start())

    doc_cols = jnp.transpose(jnp.broadcast_to(docs, (LANES, span)))
    lse_cols[...] = doc_cols
    loads[3].wait()
    for turn in range(n_head):
        dest = flip(head, n_head - 1 - turn)
        rows = pl.ds(pl.multiple_of(dest * piece, piece), piece)
        for group in range(groups):
            q_rows[turn, pl.ds(group * piece, piece), :] = q_in[
                rows, pl.ds(group * head_dim, head_dim)
            ]
        row_doc[turn] = lse_cols[rows, :]
        row_at[turn] = dest * piece + lax.broadcasted_iota(jnp.int32, (piece, LANES), 0)

    def attend(turn, k_ref, v_ref, diagonal):
        key_docs = k_ref[pl.ds(span, tail), :].astype(jnp.float32)
        biases = []
        for at in range(span // LANES):
            seen = row_doc[turn] == key_docs[at : at + 1, :]
            if diagonal:
                key_at = at * LANES + lax.broadcasted_iota(jnp.int32, (piece, LANES), 1)
                seen = seen & (key_at <= row_at[turn])
            biases.append(jnp.where(seen, 0.0, MASKED))
        bias = jnp.concatenate(biases, axis=1)
        scores = lax.dot_general(
            q_rows[turn],
            k_ref[pl.ds(0, span), :],
            (((1,), (1,)), ((), ())),
            preferred_element_type=jnp.float32,
        )
        scores = scores * scale + jnp.concatenate([bias] * groups, axis=0)
        top = jnp.max(scores, axis=1, keepdims=True)
        top = jnp.broadcast_to(top, (groups * piece, LANES))
        if not diagonal:
            old = run_max[turn]
            top = jnp.maximum(top, old)
        weights = [
            jnp.exp2(scores[:, at : at + LANES] - top) for at in range(0, span, LANES)
        ]
        total = functools.reduce(jnp.add, weights)
        mixed = jnp.dot(
            jnp.concatenate([w.astype(jnp.bfloat16) for w in weights], axis=1),
            v_ref[...],
            preferred_element_type=jnp.float32,
        )
        run_max[turn] = top
        if diagonal:
            run_sum[turn] = total
            run_acc[turn] = mixed
        else:
            factor = jnp.exp2(old - top)
            run_sum[turn] = run_sum[turn] * factor + total
            run_acc[turn] = run_acc[turn] * factor + mixed

    def attend_all(k_ref, v_ref, diagonal=False):
        def step(turn, carry):
            attend(turn, k_ref, v_ref, diagonal)
            return carry

        lax.fori_loop(0, n_head, step, 0, unroll=min(4, n_head))

    attend_all(own_k, own_v, True)

    def y_there(hop):
        return pair + side >= hop

    for hop in range(1, hops + 1):

        @pl.when(pair >= hop)
        def _():
            z_copy(hop, 0).wait_recv()

        sends(hop, 0, lambda copy: copy.start())
        if hop > 1:

            @pl.when(y_there(hop - 1))
            def _():
                for part in range(2):
                    y_copy(0, hop - 1, part).wait_recv()
                attend_all(y_k.at[hop - 2], y_v.at[hop - 2])

        @pl.when(pair >= hop)
        def _():
            z_copy(hop, 1).wait_recv()

        sends(hop, 1, lambda copy: copy.start())

        @pl.when(pair >= hop)
        def _():
            attend_all(z_k.at[hop - 1], z_v.at[hop - 1])

    @pl.when(y_there(hops))
    def _():
        for part in range(2):
            y_copy(0, hops, part).wait_recv()

    def out_copy(turn, slot):
        return pltpu.make_async_remote_copy(
            src_ref=stage.at[turn],
            dst_ref=out_ref.at[slot],
            send_sem=o_send.at[turn],
            recv_sem=o_recv.at[turn],
            device_id={"head": flip(head, n_head - 1 - turn)},
            device_id_type=MESH,
        )

    own_copy = pltpu.make_async_copy(stage.at[n_head - 1], out_ref.at[head], in_sem.at[0])
    lse_copy = pltpu.make_async_copy(lse_rows, lse_ref, in_sem.at[1])
    lane = lax.broadcasted_iota(jnp.int32, (piece, LANES), 1)
    for turn in range(n_head):

        @pl.when(y_there(hops))
        def _():
            attend(turn, y_k.at[hops - 1], y_v.at[hops - 1], False)

        dest = flip(head, n_head - 1 - turn)
        total = jnp.sum(run_sum[turn], axis=1, keepdims=True)
        total = jnp.broadcast_to(total, (groups * piece, LANES))
        normed = (run_acc[turn] * (1.0 / total)).astype(jnp.bfloat16)
        for group in range(groups):
            block = normed[group * piece : (group + 1) * piece]
            columns = pl.ds(group * head_dim, head_dim)
            stage[turn, :, columns] = block
        if turn < n_head - 1:
            out_copy(turn, head).start()
        else:
            own_copy.start()
        log_sum = run_max[turn] * math.log(2.0) + jnp.log(total)
        columns = jnp.zeros((piece, LANES), jnp.float32)
        for group in range(groups):
            columns = jnp.where(
                lane == group, log_sum[group * piece : (group + 1) * piece], columns
            )
        lse_cols[pl.ds(pl.multiple_of(dest * piece, piece), piece), :] = columns

    lse_rows[...] = jnp.transpose(lse_cols[...])[:groups]
    lse_copy.start()

    own_copy.wait()
    lse_copy.wait()
    for held in range(hops + 1):
        for part in range(2):
            sends(held, part, lambda copy: copy.wait_send())
    for turn in range(n_head - 1):
        out_copy(turn, head).wait_send()
    for turn in range(n_head - 1):
        out_copy(turn, flip(head, n_head - 1 - turn)).wait_recv()


def hand_over(out_from, lse_from, out_to, lse_to, sem):
    copies = [
        pltpu.make_async_copy(out_from.at[at], out_to.at[at], sem.at[at])
        for at in range(out_from.shape[0])
    ]
    copies.append(pltpu.make_async_copy(lse_from, lse_to.at[0], sem.at[len(copies)]))
    for copy in copies:
        copy.start()
    for copy in copies:
        copy.wait()


def body(n_ctx, n_head, queries, keys, values, documents):
    span, width = queries.shape[1:]
    head_dim = keys.shape[2]
    groups = width // head_dim
    piece, hops, tail = span // n_head, n_ctx // 4, 16
    hbm = pl.BlockSpec(memory_space=pltpu.HBM)
    bf16, f32 = jnp.bfloat16, jnp.float32
    stacked = (n_head, groups * piece, LANES)
    out, lse = pl.pallas_call(
        functools.partial(kernel, n_ctx, n_head),
        out_shape=(
            jax.ShapeDtypeStruct((n_head, piece, width), bf16),
            jax.ShapeDtypeStruct((groups, span), f32),
        ),
        in_specs=[hbm] * 4,
        out_specs=(hbm, hbm),
        scratch_shapes=[
            pltpu.VMEM((1, span), jnp.int32),
            pltpu.VMEM((span, width), bf16),
            pltpu.VMEM((n_head, groups * piece, head_dim), bf16),
            pltpu.VMEM((n_head, piece, LANES), f32),
            pltpu.VMEM((n_head, piece, LANES), jnp.int32),
            pltpu.VMEM((span + tail, head_dim), bf16),
            pltpu.VMEM((span, head_dim), bf16),
            pltpu.VMEM((hops, span + tail, head_dim), bf16),
            pltpu.VMEM((hops, span, head_dim), bf16),
            pltpu.VMEM((hops, span + tail, head_dim), bf16),
            pltpu.VMEM((hops, span, head_dim), bf16),
            pltpu.VMEM(stacked, f32),
            pltpu.VMEM(stacked, f32),
            pltpu.VMEM(stacked, f32),
            pltpu.VMEM((n_head, piece, width), bf16),
            pltpu.VMEM((span, LANES), f32),
            pltpu.VMEM((groups, span), f32),
            pltpu.SemaphoreType.DMA((4,)),
            pltpu.SemaphoreType.DMA((hops, 2)),
            pltpu.SemaphoreType.DMA((hops, 2)),
            pltpu.SemaphoreType.DMA((hops, 2)),
            pltpu.SemaphoreType.DMA((hops, 2)),
            pltpu.SemaphoreType.DMA((n_head,)),
            pltpu.SemaphoreType.DMA((n_head,)),
        ],
        compiler_params=pltpu.CompilerParams(
            collective_id=0, has_side_effects=True, vmem_limit_bytes=VMEM_GRANT
        ),
        cost_estimate=pl.CostEstimate(
            flops=2 * 2 * span * width * span * (2 * hops + 1),
            bytes_accessed=4 * span * width,
            transcendentals=span * groups * span * (2 * hops + 1),
        ),
    )(queries[0], keys[0], values[0], documents)
    out, lse = pl.pallas_call(
        hand_over,
        out_shape=(
            jax.ShapeDtypeStruct((n_head, piece, width), bf16),
            jax.ShapeDtypeStruct((1, groups, span), f32),
        ),
        in_specs=[hbm, hbm],
        out_specs=(hbm, hbm),
        scratch_shapes=[pltpu.SemaphoreType.DMA((n_head + 1,))],
        compiler_params=pltpu.CompilerParams(vmem_limit_bytes=VMEM_GRANT),
    )(out, lse)
    return out, lse


def solution(mesh):
    n_ctx, n_head = mesh.shape["ctx"], mesh.shape["head"]
    in_specs = (
        P("head", "ctx", None),
        P("head", "ctx", None),
        P("head", "ctx", None),
        P("head", "ctx"),
    )
    out_specs = (P(None, ("ctx", "head"), None), P("head", None, "ctx"))
    return jax.shard_map(
        functools.partial(body, n_ctx, n_head),
        mesh=mesh,
        in_specs=in_specs,
        out_specs=out_specs,
        check_vma=False,
    )
```

```python
import functools
import math

import jax
import jax.numpy as jnp
from jax import lax
from jax.experimental import pallas as pl
from jax.experimental.pallas import tpu as pltpu
from jax.sharding import PartitionSpec as P

MASKED = -1e30
LANES = 128
VMEM_GRANT = 63 * 1024 * 1024
MESH = pl.DeviceIdType.MESH


def flip(index, mask):
    out = index
    bit = 1
    while bit <= mask:
        if mask & bit:
            out = out + bit * (1 - 2 * (lax.rem(lax.div(index, bit), 2)))
        bit *= 2
    return out


def kernel(
    n_ctx,
    n_head,
    q_hbm,
    k_hbm,
    v_hbm,
    doc_hbm,
    out_ref,
    lse_ref,
    doc_ref,
    q_in,
    q_rows,
    row_doc,
    row_at,
    own_k,
    own_v,
    z_k,
    z_v,
    y_k,
    y_v,
    run_max,
    run_sum,
    run_acc,
    stage,
    lse_cols,
    lse_rows,
    in_sem,
    z_send,
    z_recv,
    y_send,
    y_recv,
    o_send,
    o_recv,
):
    span = own_v.shape[0]
    head_dim = own_v.shape[1]
    groups = q_in.shape[1] // head_dim
    piece = span // n_head
    pairs, hops = n_ctx // 2, n_ctx // 4
    scale = math.log2(math.e) / math.sqrt(head_dim)

    me = lax.axis_index("ctx")
    head = lax.axis_index("head")
    pair, side = lax.div(me, 2), lax.rem(me, 2)
    partner = me + 1 - 2 * side
    up, down = me + 2, me - 2
    has_up, has_down = pair + 1 < pairs, pair > 0

    loads = [
        pltpu.make_async_copy(k_hbm, own_k.at[pl.ds(0, span)], in_sem.at[0]),
        pltpu.make_async_copy(v_hbm, own_v, in_sem.at[1]),
        pltpu.make_async_copy(doc_hbm, doc_ref, in_sem.at[2]),
        pltpu.make_async_copy(q_hbm, q_in, in_sem.at[3]),
    ]
    for load in loads:
        load.start()
    barrier = pltpu.get_barrier_semaphore()

    @pl.when(has_up)
    def _():
        pl.semaphore_signal(barrier, inc=1, device_id={"ctx": up}, device_id_type=MESH)

    @pl.when(has_down)
    def _():
        pl.semaphore_signal(barrier, inc=1, device_id={"ctx": down}, device_id_type=MESH)

    pl.semaphore_signal(barrier, inc=1, device_id={"ctx": partner}, device_id_type=MESH)
    for mask in range(1, n_head):
        pl.semaphore_signal(
            barrier, inc=1, device_id={"head": flip(head, mask)}, device_id_type=MESH
        )

    loads[2].wait()
    docs = doc_ref[...].astype(jnp.float32)
    tail = own_k.shape[0] - span
    doc_tile = jnp.concatenate(
        [docs[:, at : at + LANES] for at in range(0, span, LANES)]
        + [jnp.zeros((tail - span // LANES, LANES), jnp.float32)],
        axis=0,
    )
    own_k[pl.ds(span, tail), :] = doc_tile.astype(jnp.bfloat16)
    loads[0].wait()
    loads[1].wait()
    pl.semaphore_wait(barrier, n_head + has_up.astype(jnp.int32) + has_down.astype(jnp.int32))

    def z_copy(hop, part):
        if part == 0:
            source = own_k if hop == 1 else z_k.at[hop - 2]
            target = z_k.at[hop - 1]
        else:
            source = own_v if hop == 1 else z_v.at[hop - 2]
            target = z_v.at[hop - 1]
        return pltpu.make_async_remote_copy(
            src_ref=source,
            dst_ref=target,
            send_sem=z_send.at[hop - 1, part],
            recv_sem=z_recv.at[hop - 1, part],
            device_id={"ctx": up},
            device_id_type=MESH,
        )

    def y_copy(held, hop, part):
        if part == 0:
            source = own_k if held == 0 else z_k.at[held - 1]
            target = y_k.at[hop - 1]
        else:
            source = own_v if held == 0 else z_v.at[held - 1]
            target = y_v.at[hop - 1]
        return pltpu.make_async_remote_copy(
            src_ref=source,
            dst_ref=target,
            send_sem=y_send.at[hop - 1, part],
            recv_sem=y_recv.at[hop - 1, part],
            device_id={"ctx": partner},
            device_id_type=MESH,
        )

    def sends(held, part, act):
        if held < hops:

            @pl.when(has_up & (pair >= held))
            def _():
                act(z_copy(held + 1, part))

            @pl.when((side == 0) & (pair >= held))
            def _():
                act(y_copy(held, held + 1, part))

        if held > 0:

            @pl.when((side == 1) & (pair >= held))
            def _():
                act(y_copy(held, held, part))

    for part in range(2):
        sends(0, part, lambda copy: copy.start())

    doc_cols = jnp.transpose(jnp.broadcast_to(docs, (LANES, span)))
    lse_cols[...] = doc_cols
    loads[3].wait()
    for turn in range(n_head):
        dest = flip(head, n_head - 1 - turn)
        rows = pl.ds(pl.multiple_of(dest * piece, piece), piece)
        for group in range(groups):
            q_rows[turn, pl.ds(group * piece, piece), :] = q_in[
                rows, pl.ds(group * head_dim, head_dim)
            ]
        row_doc[turn] = lse_cols[rows, :]
        row_at[turn] = dest * piece + lax.broadcasted_iota(jnp.int32, (piece, LANES), 0)

    def attend(turn, k_ref, v_ref, diagonal):
        key_docs = k_ref[pl.ds(span, tail), :].astype(jnp.float32)
        biases = []
        for at in range(span // LANES):
            seen = row_doc[turn] == key_docs[at : at + 1, :]
            if diagonal:
                key_at = at * LANES + lax.broadcasted_iota(jnp.int32, (piece, LANES), 1)
                seen = seen & (key_at <= row_at[turn])
            biases.append(jnp.where(seen, 0.0, MASKED))
        bias = jnp.concatenate(biases, axis=1)
        scores = lax.dot_general(
            q_rows[turn],
            k_ref[pl.ds(0, span), :],
            (((1,), (1,)), ((), ())),
            preferred_element_type=jnp.float32,
        )
        scores = scores * scale + jnp.concatenate([bias] * groups, axis=0)
        top = jnp.max(scores, axis=1, keepdims=True)
        top = jnp.broadcast_to(top, (groups * piece, LANES))
        if not diagonal:
            old = run_max[turn]
            top = jnp.maximum(top, old)
        weights = [
            jnp.exp2(scores[:, at : at + LANES] - top) for at in range(0, span, LANES)
        ]
        total = functools.reduce(jnp.add, weights)
        mixed = jnp.dot(
            jnp.concatenate([w.astype(jnp.bfloat16) for w in weights], axis=1),
            v_ref[...],
            preferred_element_type=jnp.float32,
        )
        run_max[turn] = top
        if diagonal:
            run_sum[turn] = total
            run_acc[turn] = mixed
        else:
            factor = jnp.exp2(old - top)
            run_sum[turn] = run_sum[turn] * factor + total
            run_acc[turn] = run_acc[turn] * factor + mixed

    def attend_all(k_ref, v_ref, diagonal=False):
        def step(turn, carry):
            attend(turn, k_ref, v_ref, diagonal)
            return carry

        lax.fori_loop(0, n_head, step, 0, unroll=min(4, n_head))

    attend_all(own_k, own_v, True)

    def y_there(hop):
        return pair + side >= hop

    for hop in range(1, hops + 1):

        @pl.when(pair >= hop)
        def _():
            z_copy(hop, 0).wait_recv()

        sends(hop, 0, lambda copy: copy.start())
        if hop > 1:

            @pl.when(y_there(hop - 1))
            def _():
                for part in range(2):
                    y_copy(0, hop - 1, part).wait_recv()
                attend_all(y_k.at[hop - 2], y_v.at[hop - 2])

        @pl.when(pair >= hop)
        def _():
            z_copy(hop, 1).wait_recv()

        sends(hop, 1, lambda copy: copy.start())

        @pl.when(pair >= hop)
        def _():
            attend_all(z_k.at[hop - 1], z_v.at[hop - 1])

    @pl.when(y_there(hops))
    def _():
        for part in range(2):
            y_copy(0, hops, part).wait_recv()

    def out_copy(turn, slot):
        return pltpu.make_async_remote_copy(
            src_ref=stage.at[turn],
            dst_ref=out_ref.at[slot],
            send_sem=o_send.at[turn],
            recv_sem=o_recv.at[turn],
            device_id={"head": flip(head, n_head - 1 - turn)},
            device_id_type=MESH,
        )

    own_copy = pltpu.make_async_copy(stage.at[n_head - 1], out_ref.at[head], in_sem.at[0])
    lse_copy = pltpu.make_async_copy(lse_rows, lse_ref, in_sem.at[1])
    lane = lax.broadcasted_iota(jnp.int32, (piece, LANES), 1)
    for turn in range(n_head):

        @pl.when(y_there(hops))
        def _():
            attend(turn, y_k.at[hops - 1], y_v.at[hops - 1], False)

        dest = flip(head, n_head - 1 - turn)
        total = jnp.sum(run_sum[turn], axis=1, keepdims=True)
        total = jnp.broadcast_to(total, (groups * piece, LANES))
        normed = (run_acc[turn] * (1.0 / total)).astype(jnp.bfloat16)
        for group in range(groups):
            block = normed[group * piece : (group + 1) * piece]
            columns = pl.ds(group * head_dim, head_dim)
            stage[turn, :, columns] = block
        if turn < n_head - 1:
            out_copy(turn, head).start()
        else:
            own_copy.start()
        log_sum = run_max[turn] * math.log(2.0) + jnp.log(total)
        columns = jnp.zeros((piece, LANES), jnp.float32)
        for group in range(groups):
            columns = jnp.where(
                lane == group, log_sum[group * piece : (group + 1) * piece], columns
            )
        lse_cols[pl.ds(pl.multiple_of(dest * piece, piece), piece), :] = columns

    lse_rows[...] = jnp.transpose(lse_cols[...])[:groups]
    lse_copy.start()

    own_copy.wait()
    lse_copy.wait()
    for held in range(hops + 1):
        for part in range(2):
            sends(held, part, lambda copy: copy.wait_send())
    for turn in range(n_head - 1):
        out_copy(turn, head).wait_send()
    for turn in range(n_head - 1):
        out_copy(turn, flip(head, n_head - 1 - turn)).wait_recv()


def hand_over(out_from, lse_from, out_to, lse_to, out_held, lse_held, in_sem, out_sem):
    count = out_from.shape[0]
    froms = [out_from.at[at] for at in range(count)] + [lse_from]
    helds = [out_held.at[at] for at in range(count)] + [lse_held]
    tos = [out_to.at[at] for at in range(count)] + [lse_to.at[0]]
    ins = [
        pltpu.make_async_copy(froms[at], helds[at], in_sem.at[at]) for at in range(count + 1)
    ]
    outs = [
        pltpu.make_async_copy(helds[at], tos[at], out_sem.at[at]) for at in range(count + 1)
    ]
    for copy in ins:
        copy.start()
    for at in range(count + 1):
        ins[at].wait()
        outs[at].start()
    for copy in outs:
        copy.wait()


def body(n_ctx, n_head, queries, keys, values, documents):
    span, width = queries.shape[1:]
    head_dim = keys.shape[2]
    groups = width // head_dim
    piece, hops, tail = span // n_head, n_ctx // 4, 16
    hbm = pl.BlockSpec(memory_space=pltpu.HBM)
    bf16, f32 = jnp.bfloat16, jnp.float32
    stacked = (n_head, groups * piece, LANES)
    out, lse = pl.pallas_call(
        functools.partial(kernel, n_ctx, n_head),
        out_shape=(
            jax.ShapeDtypeStruct((n_head, piece, width), bf16),
            jax.ShapeDtypeStruct((groups, span), f32),
        ),
        in_specs=[hbm] * 4,
        out_specs=(hbm, hbm),
        scratch_shapes=[
            pltpu.VMEM((1, span), jnp.int32),
            pltpu.VMEM((span, width), bf16),
            pltpu.VMEM((n_head, groups * piece, head_dim), bf16),
            pltpu.VMEM((n_head, piece, LANES), f32),
            pltpu.VMEM((n_head, piece, LANES), jnp.int32),
            pltpu.VMEM((span + tail, head_dim), bf16),
            pltpu.VMEM((span, head_dim), bf16),
            pltpu.VMEM((hops, span + tail, head_dim), bf16),
            pltpu.VMEM((hops, span, head_dim), bf16),
            pltpu.VMEM((hops, span + tail, head_dim), bf16),
            pltpu.VMEM((hops, span, head_dim), bf16),
            pltpu.VMEM(stacked, f32),
            pltpu.VMEM(stacked, f32),
            pltpu.VMEM(stacked, f32),
            pltpu.VMEM((n_head, piece, width), bf16),
            pltpu.VMEM((span, LANES), f32),
            pltpu.VMEM((groups, span), f32),
            pltpu.SemaphoreType.DMA((4,)),
            pltpu.SemaphoreType.DMA((hops, 2)),
            pltpu.SemaphoreType.DMA((hops, 2)),
            pltpu.SemaphoreType.DMA((hops, 2)),
            pltpu.SemaphoreType.DMA((hops, 2)),
            pltpu.SemaphoreType.DMA((n_head,)),
            pltpu.SemaphoreType.DMA((n_head,)),
        ],
        compiler_params=pltpu.CompilerParams(
            collective_id=0, has_side_effects=True, vmem_limit_bytes=VMEM_GRANT
        ),
        cost_estimate=pl.CostEstimate(
            flops=2 * 2 * span * width * span * (2 * hops + 1),
            bytes_accessed=4 * span * width,
            transcendentals=span * groups * span * (2 * hops + 1),
        ),
    )(queries[0], keys[0], values[0], documents)
    out, lse = pl.pallas_call(
        hand_over,
        out_shape=(
            jax.ShapeDtypeStruct((n_head, piece, width), bf16),
            jax.ShapeDtypeStruct((1, groups, span), f32),
        ),
        in_specs=[hbm, hbm],
        out_specs=(hbm, hbm),
        scratch_shapes=[
            pltpu.VMEM((n_head, piece, width), bf16),
            pltpu.VMEM((groups, span), f32),
            pltpu.SemaphoreType.DMA((n_head + 1,)),
            pltpu.SemaphoreType.DMA((n_head + 1,)),
        ],
        compiler_params=pltpu.CompilerParams(vmem_limit_bytes=VMEM_GRANT),
    )(out, lse)
    return out, lse


def solution(mesh):
    n_ctx, n_head = mesh.shape["ctx"], mesh.shape["head"]
    in_specs = (
        P("head", "ctx", None),
        P("head", "ctx", None),
        P("head", "ctx", None),
        P("head", "ctx"),
    )
    out_specs = (P(None, ("ctx", "head"), None), P("head", None, "ctx"))
    return jax.shard_map(
        functools.partial(body, n_ctx, n_head),
        mesh=mesh,
        in_specs=in_specs,
        out_specs=out_specs,
        check_vma=False,
    )
```

```python
import functools
import math

import jax
import jax.numpy as jnp
from jax import lax
from jax.experimental import pallas as pl
from jax.experimental.pallas import tpu as pltpu
from jax.sharding import PartitionSpec as P

MASKED = -1e30
LANES = 128
VMEM_GRANT = 63 * 1024 * 1024
MESH = pl.DeviceIdType.MESH


def flip(index, mask):
    out = index
    bit = 1
    while bit <= mask:
        if mask & bit:
            out = out + bit * (1 - 2 * (lax.rem(lax.div(index, bit), 2)))
        bit *= 2
    return out


def kernel(
    n_ctx,
    n_head,
    q_hbm,
    k_hbm,
    v_hbm,
    doc_hbm,
    out_ref,
    lse_ref,
    doc_ref,
    q_in,
    q_rows,
    row_doc,
    row_at,
    own_k,
    own_v,
    z_k,
    z_v,
    y_k,
    y_v,
    run_max,
    run_sum,
    run_acc,
    stage,
    lse_cols,
    lse_rows,
    in_sem,
    z_send,
    z_recv,
    y_send,
    y_recv,
    o_send,
    o_recv,
):
    span = own_v.shape[0]
    head_dim = own_v.shape[1]
    groups = q_in.shape[1] // head_dim
    piece = span // n_head
    pairs, hops = n_ctx // 2, n_ctx // 4
    scale = math.log2(math.e) / math.sqrt(head_dim)

    me = lax.axis_index("ctx")
    head = lax.axis_index("head")
    pair, side = lax.div(me, 2), lax.rem(me, 2)
    partner = me + 1 - 2 * side
    up, down = me + 2, me - 2
    has_up, has_down = pair + 1 < pairs, pair > 0

    loads = [
        pltpu.make_async_copy(k_hbm, own_k.at[pl.ds(0, span)], in_sem.at[0]),
        pltpu.make_async_copy(v_hbm, own_v, in_sem.at[1]),
        pltpu.make_async_copy(doc_hbm, doc_ref, in_sem.at[2]),
        pltpu.make_async_copy(q_hbm, q_in, in_sem.at[3]),
    ]
    for load in loads:
        load.start()
    barrier = pltpu.get_barrier_semaphore()

    @pl.when(has_up)
    def _():
        pl.semaphore_signal(barrier, inc=1, device_id={"ctx": up}, device_id_type=MESH)

    @pl.when(has_down)
    def _():
        pl.semaphore_signal(barrier, inc=1, device_id={"ctx": down}, device_id_type=MESH)

    pl.semaphore_signal(barrier, inc=1, device_id={"ctx": partner}, device_id_type=MESH)
    for mask in range(1, n_head):
        pl.semaphore_signal(
            barrier, inc=1, device_id={"head": flip(head, mask)}, device_id_type=MESH
        )

    loads[2].wait()
    docs = doc_ref[...].astype(jnp.float32)
    tail = own_k.shape[0] - span
    doc_tile = jnp.concatenate(
        [docs[:, at : at + LANES] for at in range(0, span, LANES)]
        + [jnp.zeros((tail - span // LANES, LANES), jnp.float32)],
        axis=0,
    )
    own_k[pl.ds(span, tail), :] = doc_tile.astype(jnp.bfloat16)
    loads[0].wait()
    loads[1].wait()
    pl.semaphore_wait(barrier, n_head + has_up.astype(jnp.int32) + has_down.astype(jnp.int32))

    half = span // 2
    parts = ((0, half), (half, half + tail), (0, half), (half, half))

    def source_of(held, part):
        which, rows = part // 2, pl.ds(*parts[part])
        if held == 0:
            return (own_k, own_v)[which].at[rows]
        return (z_k, z_v)[which].at[held - 1, rows]

    def z_copy(hop, part):
        return pltpu.make_async_remote_copy(
            src_ref=source_of(hop - 1, part),
            dst_ref=(z_k, z_v)[part // 2].at[hop - 1, pl.ds(*parts[part])],
            send_sem=z_send.at[hop - 1, part],
            recv_sem=z_recv.at[hop - 1, part],
            device_id={"ctx": up},
            device_id_type=MESH,
        )

    def y_copy(held, hop, part):
        return pltpu.make_async_remote_copy(
            src_ref=source_of(held, part),
            dst_ref=(y_k, y_v)[part // 2].at[hop - 1, pl.ds(*parts[part])],
            send_sem=y_send.at[hop - 1, part],
            recv_sem=y_recv.at[hop - 1, part],
            device_id={"ctx": partner},
            device_id_type=MESH,
        )

    def sends(held, part, act):
        if held < hops:

            @pl.when(has_up & (pair >= held))
            def _():
                act(z_copy(held + 1, part))

            @pl.when((side == 0) & (pair >= held))
            def _():
                act(y_copy(held, held + 1, part))

        if held > 0:

            @pl.when((side == 1) & (pair >= held))
            def _():
                act(y_copy(held, held, part))

    for part in range(len(parts)):
        sends(0, part, lambda copy: copy.start())

    doc_cols = jnp.transpose(jnp.broadcast_to(docs, (LANES, span)))
    lse_cols[...] = doc_cols
    loads[3].wait()
    for turn in range(n_head):
        dest = flip(head, n_head - 1 - turn)
        rows = pl.ds(pl.multiple_of(dest * piece, piece), piece)
        for group in range(groups):
            q_rows[turn, pl.ds(group * piece, piece), :] = q_in[
                rows, pl.ds(group * head_dim, head_dim)
            ]
        row_doc[turn] = lse_cols[rows, :]
        row_at[turn] = dest * piece + lax.broadcasted_iota(jnp.int32, (piece, LANES), 0)

    def attend(turn, k_ref, v_ref, diagonal):
        key_docs = k_ref[pl.ds(span, tail), :].astype(jnp.float32)
        biases = []
        for at in range(span // LANES):
            seen = row_doc[turn] == key_docs[at : at + 1, :]
            if diagonal:
                key_at = at * LANES + lax.broadcasted_iota(jnp.int32, (piece, LANES), 1)
                seen = seen & (key_at <= row_at[turn])
            biases.append(jnp.where(seen, 0.0, MASKED))
        bias = jnp.concatenate(biases, axis=1)
        scores = lax.dot_general(
            q_rows[turn],
            k_ref[pl.ds(0, span), :],
            (((1,), (1,)), ((), ())),
            preferred_element_type=jnp.float32,
        )
        scores = scores * scale + jnp.concatenate([bias] * groups, axis=0)
        top = jnp.max(scores, axis=1, keepdims=True)
        top = jnp.broadcast_to(top, (groups * piece, LANES))
        if not diagonal:
            old = run_max[turn]
            top = jnp.maximum(top, old)
        weights = [
            jnp.exp2(scores[:, at : at + LANES] - top) for at in range(0, span, LANES)
        ]
        total = functools.reduce(jnp.add, weights)
        mixed = jnp.dot(
            jnp.concatenate([w.astype(jnp.bfloat16) for w in weights], axis=1),
            v_ref[...],
            preferred_element_type=jnp.float32,
        )
        if diagonal:
            return top, total, mixed
        factor = jnp.exp2(old - top)
        return top, run_sum[turn] * factor + total, run_acc[turn] * factor + mixed

    def attend_some(first, last, k_ref, v_ref, diagonal=False):
        def step(turn, carry):
            run_max[turn], run_sum[turn], run_acc[turn] = attend(turn, k_ref, v_ref, diagonal)
            return carry

        lax.fori_loop(first, last, step, 0, unroll=min(4, last - first))

    def y_there(hop):
        return pair + side >= hop

    middle = n_head // 2
    spans = ((0, middle), (middle, n_head))

    def own_half(at):
        attend_some(*spans[at], own_k, own_v, True)

    def z_half(hop, at):
        @pl.when(pair >= hop)
        def _():
            attend_some(*spans[at], z_k.at[hop - 1], z_v.at[hop - 1])

    def y_half(hop, at):
        @pl.when(y_there(hop))
        def _():
            if at == 0:
                y_wait(hop)
            attend_some(*spans[at], y_k.at[hop - 1], y_v.at[hop - 1])

    def y_wait(hop):
        for part in range(len(parts)):
            y_copy(0, hop, part).wait_recv()

    def pass_on(hop, part):
        @pl.when(pair >= hop)
        def _():
            z_copy(hop, part).wait_recv()

        sends(hop, part, lambda copy: copy.start())

    for hop in range(1, hops + 1):
        if hop == 1:
            own_half(0)
            pass_on(1, 0)
            own_half(1)
            for part in range(1, len(parts)):
                pass_on(1, part)
        else:
            for at in range(2):
                z_half(hop - 1, at)
                pass_on(hop, at)
            for at in range(2):
                y_half(hop - 1, at)
                pass_on(hop, 2 + at)
    for at in range(2):
        z_half(hops, at)

    def out_copy(turn, slot):
        return pltpu.make_async_remote_copy(
            src_ref=stage.at[turn],
            dst_ref=out_ref.at[slot],
            send_sem=o_send.at[turn],
            recv_sem=o_recv.at[turn],
            device_id={"head": flip(head, n_head - 1 - turn)},
            device_id_type=MESH,
        )

    own_copy = pltpu.make_async_copy(stage.at[n_head - 1], out_ref.at[head], in_sem.at[0])
    lse_copy = pltpu.make_async_copy(lse_rows, lse_ref, in_sem.at[1])
    def finish(turn, sums):
        top, total, mixed = sums
        total = jnp.broadcast_to(
            jnp.sum(total, axis=1, keepdims=True), (groups * piece, LANES)
        )
        normed = (mixed * (1.0 / total)).astype(jnp.bfloat16)
        for group in range(groups):
            stage[turn, :, pl.ds(group * head_dim, head_dim)] = normed[
                group * piece : (group + 1) * piece
            ]
        if turn < n_head - 1:
            out_copy(turn, head).start()
        else:
            own_copy.start()
        run_max[turn] = top
        run_sum[turn] = total

    @pl.when(y_there(hops))
    def _():
        y_wait(hops)
        for turn in range(n_head):
            finish(turn, attend(turn, y_k.at[hops - 1], y_v.at[hops - 1], False))

    @pl.when(pair + side < hops)
    def _():
        for turn in range(n_head):
            finish(turn, (run_max[turn], run_sum[turn], run_acc[turn]))

    lane = lax.broadcasted_iota(jnp.int32, (piece, LANES), 1)
    for turn in range(n_head):
        dest = flip(head, n_head - 1 - turn)
        log_sum = run_max[turn] * math.log(2.0) + jnp.log(run_sum[turn])
        columns = jnp.zeros((piece, LANES), jnp.float32)
        for group in range(groups):
            columns = jnp.where(
                lane == group, log_sum[group * piece : (group + 1) * piece], columns
            )
        lse_cols[pl.ds(pl.multiple_of(dest * piece, piece), piece), :] = columns

    lse_rows[...] = jnp.transpose(lse_cols[...])[:groups]
    lse_copy.start()

    own_copy.wait()
    lse_copy.wait()
    for held in range(hops + 1):
        for part in range(len(parts)):
            sends(held, part, lambda copy: copy.wait_send())
    for turn in range(n_head - 1):
        out_copy(turn, head).wait_send()
    for turn in range(n_head - 1):
        out_copy(turn, flip(head, n_head - 1 - turn)).wait_recv()


def hand_over(out_from, lse_from, out_to, lse_to, out_held, lse_held, in_sem, out_sem):
    count = out_from.shape[0]
    froms = [out_from.at[at] for at in range(count)] + [lse_from]
    helds = [out_held.at[at] for at in range(count)] + [lse_held]
    tos = [out_to.at[at] for at in range(count)] + [lse_to.at[0]]
    ins = [
        pltpu.make_async_copy(froms[at], helds[at], in_sem.at[at]) for at in range(count + 1)
    ]
    outs = [
        pltpu.make_async_copy(helds[at], tos[at], out_sem.at[at]) for at in range(count + 1)
    ]
    for copy in ins:
        copy.start()
    for at in range(count + 1):
        ins[at].wait()
        outs[at].start()
    for copy in outs:
        copy.wait()


def body(n_ctx, n_head, queries, keys, values, documents):
    span, width = queries.shape[1:]
    head_dim = keys.shape[2]
    groups = width // head_dim
    piece, hops, tail = span // n_head, n_ctx // 4, 16
    hbm = pl.BlockSpec(memory_space=pltpu.HBM)
    bf16, f32 = jnp.bfloat16, jnp.float32
    stacked = (n_head, groups * piece, LANES)
    out, lse = pl.pallas_call(
        functools.partial(kernel, n_ctx, n_head),
        out_shape=(
            jax.ShapeDtypeStruct((n_head, piece, width), bf16),
            jax.ShapeDtypeStruct((groups, span), f32),
        ),
        in_specs=[hbm] * 4,
        out_specs=(hbm, hbm),
        scratch_shapes=[
            pltpu.VMEM((1, span), jnp.int32),
            pltpu.VMEM((span, width), bf16),
            pltpu.VMEM((n_head, groups * piece, head_dim), bf16),
            pltpu.VMEM((n_head, piece, LANES), f32),
            pltpu.VMEM((n_head, piece, LANES), jnp.int32),
            pltpu.VMEM((span + tail, head_dim), bf16),
            pltpu.VMEM((span, head_dim), bf16),
            pltpu.VMEM((hops, span + tail, head_dim), bf16),
            pltpu.VMEM((hops, span, head_dim), bf16),
            pltpu.VMEM((hops, span + tail, head_dim), bf16),
            pltpu.VMEM((hops, span, head_dim), bf16),
            pltpu.VMEM(stacked, f32),
            pltpu.VMEM(stacked, f32),
            pltpu.VMEM(stacked, f32),
            pltpu.VMEM((n_head, piece, width), bf16),
            pltpu.VMEM((span, LANES), f32),
            pltpu.VMEM((groups, span), f32),
            pltpu.SemaphoreType.DMA((4,)),
            pltpu.SemaphoreType.DMA((hops, 4)),
            pltpu.SemaphoreType.DMA((hops, 4)),
            pltpu.SemaphoreType.DMA((hops, 4)),
            pltpu.SemaphoreType.DMA((hops, 4)),
            pltpu.SemaphoreType.DMA((n_head,)),
            pltpu.SemaphoreType.DMA((n_head,)),
        ],
        compiler_params=pltpu.CompilerParams(
            collective_id=0, has_side_effects=True, vmem_limit_bytes=VMEM_GRANT
        ),
        cost_estimate=pl.CostEstimate(
            flops=2 * 2 * span * width * span * (2 * hops + 1),
            bytes_accessed=4 * span * width,
            transcendentals=span * groups * span * (2 * hops + 1),
        ),
    )(queries[0], keys[0], values[0], documents)
    out, lse = pl.pallas_call(
        hand_over,
        out_shape=(
            jax.ShapeDtypeStruct((n_head, piece, width), bf16),
            jax.ShapeDtypeStruct((1, groups, span), f32),
        ),
        in_specs=[hbm, hbm],
        out_specs=(hbm, hbm),
        scratch_shapes=[
            pltpu.VMEM((n_head, piece, width), bf16),
            pltpu.VMEM((groups, span), f32),
            pltpu.SemaphoreType.DMA((n_head + 1,)),
            pltpu.SemaphoreType.DMA((n_head + 1,)),
        ],
        compiler_params=pltpu.CompilerParams(vmem_limit_bytes=VMEM_GRANT),
    )(out, lse)
    return out, lse


def solution(mesh):
    n_ctx, n_head = mesh.shape["ctx"], mesh.shape["head"]
    in_specs = (
        P("head", "ctx", None),
        P("head", "ctx", None),
        P("head", "ctx", None),
        P("head", "ctx"),
    )
    out_specs = (P(None, ("ctx", "head"), None), P("head", None, "ctx"))
    return jax.shard_map(
        functools.partial(body, n_ctx, n_head),
        mesh=mesh,
        in_specs=in_specs,
        out_specs=out_specs,
        check_vma=False,
    )
```

```python
import functools
import math

import jax
import jax.numpy as jnp
from jax import lax
from jax.experimental import pallas as pl
from jax.experimental.pallas import tpu as pltpu
from jax.sharding import PartitionSpec as P

MASKED = -1e30
LANES = 128
VMEM_GRANT = 63 * 1024 * 1024
MESH = pl.DeviceIdType.MESH


def flip(index, mask):
    out = index
    bit = 1
    while bit <= mask:
        if mask & bit:
            out = out + bit * (1 - 2 * (lax.rem(lax.div(index, bit), 2)))
        bit *= 2
    return out


def kernel(
    n_ctx,
    n_head,
    q_hbm,
    k_hbm,
    v_hbm,
    doc_hbm,
    out_ref,
    lse_ref,
    doc_ref,
    q_in,
    q_rows,
    row_doc,
    row_at,
    own_k,
    own_v,
    z_k,
    z_v,
    y_k,
    y_v,
    run_max,
    run_sum,
    run_acc,
    last_weights,
    stage,
    lse_cols,
    lse_rows,
    in_sem,
    z_send,
    z_recv,
    y_send,
    y_recv,
    o_send,
    o_recv,
):
    span = own_v.shape[0]
    head_dim = own_v.shape[1]
    groups = q_in.shape[1] // head_dim
    piece = span // n_head
    pairs, hops = n_ctx // 2, n_ctx // 4
    scale = math.log2(math.e) / math.sqrt(head_dim)

    me = lax.axis_index("ctx")
    head = lax.axis_index("head")
    pair, side = lax.div(me, 2), lax.rem(me, 2)
    partner = me + 1 - 2 * side
    up, down = me + 2, me - 2
    has_up, has_down = pair + 1 < pairs, pair > 0

    loads = [
        pltpu.make_async_copy(k_hbm, own_k.at[pl.ds(0, span)], in_sem.at[0]),
        pltpu.make_async_copy(v_hbm, own_v, in_sem.at[1]),
        pltpu.make_async_copy(doc_hbm, doc_ref, in_sem.at[2]),
        pltpu.make_async_copy(q_hbm, q_in, in_sem.at[3]),
    ]
    for load in loads:
        load.start()
    barrier = pltpu.get_barrier_semaphore()

    @pl.when(has_up)
    def _():
        pl.semaphore_signal(barrier, inc=1, device_id={"ctx": up}, device_id_type=MESH)

    @pl.when(has_down)
    def _():
        pl.semaphore_signal(barrier, inc=1, device_id={"ctx": down}, device_id_type=MESH)

    pl.semaphore_signal(barrier, inc=1, device_id={"ctx": partner}, device_id_type=MESH)
    for mask in range(1, n_head):
        pl.semaphore_signal(
            barrier, inc=1, device_id={"head": flip(head, mask)}, device_id_type=MESH
        )

    loads[2].wait()
    docs = doc_ref[...].astype(jnp.float32)
    tail = own_k.shape[0] - span
    doc_tile = jnp.concatenate(
        [docs[:, at : at + LANES] for at in range(0, span, LANES)]
        + [jnp.zeros((tail - span // LANES, LANES), jnp.float32)],
        axis=0,
    )
    own_k[pl.ds(span, tail), :] = doc_tile.astype(jnp.bfloat16)
    loads[0].wait()
    loads[1].wait()
    pl.semaphore_wait(barrier, n_head + has_up.astype(jnp.int32) + has_down.astype(jnp.int32))

    half = span // 2
    parts = ((0, half), (half, half + tail), (0, half), (half, half))

    def source_of(held, part):
        which, rows = part // 2, pl.ds(*parts[part])
        if held == 0:
            return (own_k, own_v)[which].at[rows]
        return (z_k, z_v)[which].at[held - 1, rows]

    def z_copy(hop, part):
        return pltpu.make_async_remote_copy(
            src_ref=source_of(hop - 1, part),
            dst_ref=(z_k, z_v)[part // 2].at[hop - 1, pl.ds(*parts[part])],
            send_sem=z_send.at[hop - 1, part],
            recv_sem=z_recv.at[hop - 1, part],
            device_id={"ctx": up},
            device_id_type=MESH,
        )

    def y_copy(held, hop, part):
        return pltpu.make_async_remote_copy(
            src_ref=source_of(held, part),
            dst_ref=(y_k, y_v)[part // 2].at[hop - 1, pl.ds(*parts[part])],
            send_sem=y_send.at[hop - 1, part],
            recv_sem=y_recv.at[hop - 1, part],
            device_id={"ctx": partner},
            device_id_type=MESH,
        )

    def sends(held, part, act):
        if held < hops:

            @pl.when(has_up & (pair >= held))
            def _():
                act(z_copy(held + 1, part))

            @pl.when((side == 0) & (pair >= held))
            def _():
                act(y_copy(held, held + 1, part))

        if held > 0:

            @pl.when((side == 1) & (pair >= held))
            def _():
                act(y_copy(held, held, part))

    for part in range(len(parts)):
        sends(0, part, lambda copy: copy.start())

    doc_cols = jnp.transpose(jnp.broadcast_to(docs, (LANES, span)))
    lse_cols[...] = doc_cols
    loads[3].wait()
    for turn in range(n_head):
        dest = flip(head, n_head - 1 - turn)
        rows = pl.ds(pl.multiple_of(dest * piece, piece), piece)
        for group in range(groups):
            q_rows[turn, pl.ds(group * piece, piece), :] = q_in[
                rows, pl.ds(group * head_dim, head_dim)
            ]
        row_doc[turn] = lse_cols[rows, :]
        row_at[turn] = dest * piece + lax.broadcasted_iota(jnp.int32, (piece, LANES), 0)

    def weigh(turn, k_ref, diagonal):
        key_docs = k_ref[pl.ds(span, tail), :].astype(jnp.float32)
        biases = []
        for at in range(span // LANES):
            seen = row_doc[turn] == key_docs[at : at + 1, :]
            if diagonal:
                key_at = at * LANES + lax.broadcasted_iota(jnp.int32, (piece, LANES), 1)
                seen = seen & (key_at <= row_at[turn])
            biases.append(jnp.where(seen, 0.0, MASKED))
        bias = jnp.concatenate(biases, axis=1)
        scores = lax.dot_general(
            q_rows[turn],
            k_ref[pl.ds(0, span), :],
            (((1,), (1,)), ((), ())),
            preferred_element_type=jnp.float32,
        )
        scores = scores * scale + jnp.concatenate([bias] * groups, axis=0)
        top = jnp.max(scores, axis=1, keepdims=True)
        top = jnp.broadcast_to(top, (groups * piece, LANES))
        if not diagonal:
            old = run_max[turn]
            top = jnp.maximum(top, old)
        weights = [
            jnp.exp2(scores[:, at : at + LANES] - top) for at in range(0, span, LANES)
        ]
        total = functools.reduce(jnp.add, weights)
        rounded = jnp.concatenate([w.astype(jnp.bfloat16) for w in weights], axis=1)
        if diagonal:
            return top, total, rounded, None
        factor = jnp.exp2(old - top)
        return top, run_sum[turn] * factor + total, rounded, factor

    def mix(rounded, v_ref):
        return jnp.dot(rounded, v_ref[...], preferred_element_type=jnp.float32)

    def attend(turn, k_ref, v_ref, diagonal):
        top, total, rounded, factor = weigh(turn, k_ref, diagonal)
        mixed = mix(rounded, v_ref)
        return top, total, mixed if diagonal else run_acc[turn] * factor + mixed

    def attend_some(first, last, k_ref, v_ref, diagonal=False):
        def step(turn, carry):
            run_max[turn], run_sum[turn], run_acc[turn] = attend(turn, k_ref, v_ref, diagonal)
            return carry

        lax.fori_loop(first, last, step, 0, unroll=min(4, last - first))

    def y_there(hop):
        return pair + side >= hop

    middle = n_head // 2
    spans = ((0, middle), (middle, n_head))

    def own_half(at):
        attend_some(*spans[at], own_k, own_v, True)

    def z_half(hop, at):
        @pl.when(pair >= hop)
        def _():
            attend_some(*spans[at], z_k.at[hop - 1], z_v.at[hop - 1])

    def y_half(hop, at):
        @pl.when(y_there(hop))
        def _():
            if at == 0:
                y_wait(hop, range(len(parts)))
            attend_some(*spans[at], y_k.at[hop - 1], y_v.at[hop - 1])

    def y_wait(hop, some):
        for part in some:
            y_copy(0, hop, part).wait_recv()

    def pass_on(hop, part):
        @pl.when(pair >= hop)
        def _():
            z_copy(hop, part).wait_recv()

        sends(hop, part, lambda copy: copy.start())

    for hop in range(1, hops + 1):
        if hop == 1:
            own_half(0)
            pass_on(1, 0)
            own_half(1)
            for part in range(1, len(parts)):
                pass_on(1, part)
        else:
            for at in range(2):
                z_half(hop - 1, at)
                pass_on(hop, at)
            @pl.when(side == 0)
            def _():
                for at in range(2):
                    y_half(hop - 1, at)

            pass_on(hop, 2)
            pass_on(hop, 3)

            @pl.when(side == 1)
            def _():
                for at in range(2):
                    y_half(hop - 1, at)

    for at in range(2):
        z_half(hops, at)

    def out_copy(turn, slot):
        return pltpu.make_async_remote_copy(
            src_ref=stage.at[turn],
            dst_ref=out_ref.at[slot],
            send_sem=o_send.at[turn],
            recv_sem=o_recv.at[turn],
            device_id={"head": flip(head, n_head - 1 - turn)},
            device_id_type=MESH,
        )

    own_copy = pltpu.make_async_copy(stage.at[n_head - 1], out_ref.at[head], in_sem.at[0])
    lse_copy = pltpu.make_async_copy(lse_rows, lse_ref, in_sem.at[1])
    def finish(turn, sums):
        top, total, mixed = sums
        total = jnp.broadcast_to(
            jnp.sum(total, axis=1, keepdims=True), (groups * piece, LANES)
        )
        normed = (mixed * (1.0 / total)).astype(jnp.bfloat16)
        for group in range(groups):
            stage[turn, :, pl.ds(group * head_dim, head_dim)] = normed[
                group * piece : (group + 1) * piece
            ]
        if turn < n_head - 1:
            out_copy(turn, head).start()
        else:
            own_copy.start()
        run_max[turn] = top
        run_sum[turn] = total

    @pl.when(y_there(hops))
    def _():
        y_wait(hops, (0, 1))
        for turn in range(n_head):
            run_max[turn], run_sum[turn], last_weights[turn], factor = weigh(
                turn, y_k.at[hops - 1], False
            )
            run_acc[turn] = run_acc[turn] * factor
        y_wait(hops, (2, 3))
        for turn in range(n_head):
            mixed = run_acc[turn] + mix(last_weights[turn], y_v.at[hops - 1])
            finish(turn, (run_max[turn], run_sum[turn], mixed))

    @pl.when(pair + side < hops)
    def _():
        for turn in range(n_head):
            finish(turn, (run_max[turn], run_sum[turn], run_acc[turn]))

    lane = lax.broadcasted_iota(jnp.int32, (piece, LANES), 1)
    for turn in range(n_head):
        dest = flip(head, n_head - 1 - turn)
        log_sum = run_max[turn] * math.log(2.0) + jnp.log(run_sum[turn])
        columns = jnp.zeros((piece, LANES), jnp.float32)
        for group in range(groups):
            columns = jnp.where(
                lane == group, log_sum[group * piece : (group + 1) * piece], columns
            )
        lse_cols[pl.ds(pl.multiple_of(dest * piece, piece), piece), :] = columns

    lse_rows[...] = jnp.transpose(lse_cols[...])[:groups]
    lse_copy.start()

    own_copy.wait()
    lse_copy.wait()
    for held in range(hops + 1):
        for part in range(len(parts)):
            sends(held, part, lambda copy: copy.wait_send())
    for turn in range(n_head - 1):
        out_copy(turn, head).wait_send()
    for turn in range(n_head - 1):
        out_copy(turn, flip(head, n_head - 1 - turn)).wait_recv()


def hand_over(out_from, lse_from, out_to, lse_to, out_held, lse_held, in_sem, out_sem):
    count = out_from.shape[0]
    froms = [out_from.at[at] for at in range(count)] + [lse_from]
    helds = [out_held.at[at] for at in range(count)] + [lse_held]
    tos = [out_to.at[at] for at in range(count)] + [lse_to.at[0]]
    ins = [
        pltpu.make_async_copy(froms[at], helds[at], in_sem.at[at]) for at in range(count + 1)
    ]
    outs = [
        pltpu.make_async_copy(helds[at], tos[at], out_sem.at[at]) for at in range(count + 1)
    ]
    for copy in ins:
        copy.start()
    for at in range(count + 1):
        ins[at].wait()
        outs[at].start()
    for copy in outs:
        copy.wait()


def body(n_ctx, n_head, queries, keys, values, documents):
    span, width = queries.shape[1:]
    head_dim = keys.shape[2]
    groups = width // head_dim
    piece, hops, tail = span // n_head, n_ctx // 4, 16
    hbm = pl.BlockSpec(memory_space=pltpu.HBM)
    bf16, f32 = jnp.bfloat16, jnp.float32
    stacked = (n_head, groups * piece, LANES)
    out, lse = pl.pallas_call(
        functools.partial(kernel, n_ctx, n_head),
        out_shape=(
            jax.ShapeDtypeStruct((n_head, piece, width), bf16),
            jax.ShapeDtypeStruct((groups, span), f32),
        ),
        in_specs=[hbm] * 4,
        out_specs=(hbm, hbm),
        scratch_shapes=[
            pltpu.VMEM((1, span), jnp.int32),
            pltpu.VMEM((span, width), bf16),
            pltpu.VMEM((n_head, groups * piece, head_dim), bf16),
            pltpu.VMEM((n_head, piece, LANES), f32),
            pltpu.VMEM((n_head, piece, LANES), jnp.int32),
            pltpu.VMEM((span + tail, head_dim), bf16),
            pltpu.VMEM((span, head_dim), bf16),
            pltpu.VMEM((hops, span + tail, head_dim), bf16),
            pltpu.VMEM((hops, span, head_dim), bf16),
            pltpu.VMEM((hops, span + tail, head_dim), bf16),
            pltpu.VMEM((hops, span, head_dim), bf16),
            pltpu.VMEM(stacked, f32),
            pltpu.VMEM(stacked, f32),
            pltpu.VMEM(stacked, f32),
            pltpu.VMEM((n_head, groups * piece, span), bf16),
            pltpu.VMEM((n_head, piece, width), bf16),
            pltpu.VMEM((span, LANES), f32),
            pltpu.VMEM((groups, span), f32),
            pltpu.SemaphoreType.DMA((4,)),
            pltpu.SemaphoreType.DMA((hops, 4)),
            pltpu.SemaphoreType.DMA((hops, 4)),
            pltpu.SemaphoreType.DMA((hops, 4)),
            pltpu.SemaphoreType.DMA((hops, 4)),
            pltpu.SemaphoreType.DMA((n_head,)),
            pltpu.SemaphoreType.DMA((n_head,)),
        ],
        compiler_params=pltpu.CompilerParams(
            collective_id=0, has_side_effects=True, vmem_limit_bytes=VMEM_GRANT
        ),
        cost_estimate=pl.CostEstimate(
            flops=2 * 2 * span * width * span * (2 * hops + 1),
            bytes_accessed=4 * span * width,
            transcendentals=span * groups * span * (2 * hops + 1),
        ),
    )(queries[0], keys[0], values[0], documents)
    out, lse = pl.pallas_call(
        hand_over,
        out_shape=(
            jax.ShapeDtypeStruct((n_head, piece, width), bf16),
            jax.ShapeDtypeStruct((1, groups, span), f32),
        ),
        in_specs=[hbm, hbm],
        out_specs=(hbm, hbm),
        scratch_shapes=[
            pltpu.VMEM((n_head, piece, width), bf16),
            pltpu.VMEM((groups, span), f32),
            pltpu.SemaphoreType.DMA((n_head + 1,)),
            pltpu.SemaphoreType.DMA((n_head + 1,)),
        ],
        compiler_params=pltpu.CompilerParams(vmem_limit_bytes=VMEM_GRANT),
    )(out, lse)
    return out, lse


def solution(mesh):
    n_ctx, n_head = mesh.shape["ctx"], mesh.shape["head"]
    in_specs = (
        P("head", "ctx", None),
        P("head", "ctx", None),
        P("head", "ctx", None),
        P("head", "ctx"),
    )
    out_specs = (P(None, ("ctx", "head"), None), P("head", None, "ctx"))
    return jax.shard_map(
        functools.partial(body, n_ctx, n_head),
        mesh=mesh,
        in_specs=in_specs,
        out_specs=out_specs,
        check_vma=False,
    )
```

```python
import functools
import math

import jax
import jax.numpy as jnp
from jax import lax
from jax.experimental import pallas as pl
from jax.experimental.pallas import tpu as pltpu
from jax.sharding import PartitionSpec as P

MASKED = -1e30
LANES = 128
VMEM_GRANT = 63 * 1024 * 1024
MESH = pl.DeviceIdType.MESH


def flip(index, mask):
    out = index
    bit = 1
    while bit <= mask:
        if mask & bit:
            out = out + bit * (1 - 2 * (lax.rem(lax.div(index, bit), 2)))
        bit *= 2
    return out


def kernel(
    n_ctx,
    n_head,
    q_hbm,
    k_hbm,
    v_hbm,
    doc_hbm,
    out_ref,
    lse_ref,
    doc_ref,
    q_in,
    q_rows,
    row_doc,
    row_at,
    own_k,
    own_v,
    z_k,
    z_v,
    y_k,
    y_v,
    run_max,
    run_sum,
    run_acc,
    stage,
    lse_cols,
    lse_rows,
    in_sem,
    z_send,
    z_recv,
    y_send,
    y_recv,
    o_send,
    o_recv,
):
    span = own_v.shape[0]
    head_dim = own_v.shape[1]
    groups = q_in.shape[1] // head_dim
    piece = span // n_head
    pairs, hops = n_ctx // 2, n_ctx // 4
    scale = math.log2(math.e) / math.sqrt(head_dim)

    me = lax.axis_index("ctx")
    head = lax.axis_index("head")
    pair, side = lax.div(me, 2), lax.rem(me, 2)
    partner = me + 1 - 2 * side
    up, down = me + 2, me - 2
    has_up, has_down = pair + 1 < pairs, pair > 0

    loads = [
        pltpu.make_async_copy(k_hbm, own_k.at[pl.ds(0, span)], in_sem.at[0]),
        pltpu.make_async_copy(v_hbm, own_v, in_sem.at[1]),
        pltpu.make_async_copy(doc_hbm, doc_ref, in_sem.at[2]),
        pltpu.make_async_copy(q_hbm, q_in, in_sem.at[3]),
    ]
    for load in loads:
        load.start()
    barrier = pltpu.get_barrier_semaphore()

    @pl.when(has_up)
    def _():
        pl.semaphore_signal(barrier, inc=1, device_id={"ctx": up}, device_id_type=MESH)

    @pl.when(has_down)
    def _():
        pl.semaphore_signal(barrier, inc=1, device_id={"ctx": down}, device_id_type=MESH)

    pl.semaphore_signal(barrier, inc=1, device_id={"ctx": partner}, device_id_type=MESH)
    for mask in range(1, n_head):
        pl.semaphore_signal(
            barrier, inc=1, device_id={"head": flip(head, mask)}, device_id_type=MESH
        )

    loads[2].wait()
    docs = doc_ref[...].astype(jnp.float32)
    tail = own_k.shape[0] - span
    doc_tile = jnp.concatenate(
        [docs[:, at : at + LANES] for at in range(0, span, LANES)]
        + [jnp.zeros((tail - span // LANES, LANES), jnp.float32)],
        axis=0,
    )
    own_k[pl.ds(span, tail), :] = doc_tile.astype(jnp.bfloat16)
    loads[0].wait()
    loads[1].wait()
    pl.semaphore_wait(barrier, n_head + has_up.astype(jnp.int32) + has_down.astype(jnp.int32))

    half = span // 2
    parts = ((0, half), (half, half + tail), (0, half), (half, half))

    def source_of(held, part):
        which, rows = part // 2, pl.ds(*parts[part])
        if held == 0:
            return (own_k, own_v)[which].at[rows]
        return (z_k, z_v)[which].at[held - 1, rows]

    def z_copy(hop, part):
        return pltpu.make_async_remote_copy(
            src_ref=source_of(hop - 1, part),
            dst_ref=(z_k, z_v)[part // 2].at[hop - 1, pl.ds(*parts[part])],
            send_sem=z_send.at[hop - 1, part],
            recv_sem=z_recv.at[hop - 1, part],
            device_id={"ctx": up},
            device_id_type=MESH,
        )

    def y_copy(held, hop, part):
        return pltpu.make_async_remote_copy(
            src_ref=source_of(held, part),
            dst_ref=(y_k, y_v)[part // 2].at[hop - 1, pl.ds(*parts[part])],
            send_sem=y_send.at[hop - 1, part],
            recv_sem=y_recv.at[hop - 1, part],
            device_id={"ctx": partner},
            device_id_type=MESH,
        )

    def sends(held, part, act):
        if held < hops:

            @pl.when(has_up & (pair >= held))
            def _():
                act(z_copy(held + 1, part))

            @pl.when((side == 0) & (pair >= held))
            def _():
                act(y_copy(held, held + 1, part))

        if held > 0:

            @pl.when((side == 1) & (pair >= held))
            def _():
                act(y_copy(held, held, part))

    for part in range(len(parts)):
        sends(0, part, lambda copy: copy.start())

    doc_cols = jnp.transpose(jnp.broadcast_to(docs, (LANES, span)))
    lse_cols[...] = doc_cols
    loads[3].wait()
    for turn in range(n_head):
        dest = flip(head, n_head - 1 - turn)
        rows = pl.ds(pl.multiple_of(dest * piece, piece), piece)
        for group in range(groups):
            q_rows[turn, pl.ds(group * piece, piece), :] = q_in[
                rows, pl.ds(group * head_dim, head_dim)
            ]
        row_doc[turn] = lse_cols[rows, :]
        row_at[turn] = dest * piece + lax.broadcasted_iota(jnp.int32, (piece, LANES), 0)

    def attend(turn, k_ref, v_ref, diagonal):
        key_docs = k_ref[pl.ds(span, tail), :].astype(jnp.float32)
        biases = []
        for at in range(span // LANES):
            seen = row_doc[turn] == key_docs[at : at + 1, :]
            if diagonal:
                key_at = at * LANES + lax.broadcasted_iota(jnp.int32, (piece, LANES), 1)
                seen = seen & (key_at <= row_at[turn])
            biases.append(jnp.where(seen, 0.0, MASKED))
        bias = jnp.concatenate(biases, axis=1)
        scores = lax.dot_general(
            q_rows[turn],
            k_ref[pl.ds(0, span), :],
            (((1,), (1,)), ((), ())),
            preferred_element_type=jnp.float32,
        )
        scores = scores * scale + jnp.concatenate([bias] * groups, axis=0)
        top = jnp.max(scores, axis=1, keepdims=True)
        top = jnp.broadcast_to(top, (groups * piece, LANES))
        if not diagonal:
            old = run_max[turn]
            top = jnp.maximum(top, old)
        weights = [
            jnp.exp2(scores[:, at : at + LANES] - top) for at in range(0, span, LANES)
        ]
        total = functools.reduce(jnp.add, weights)
        mixed = jnp.dot(
            jnp.concatenate([w.astype(jnp.bfloat16) for w in weights], axis=1),
            v_ref[...],
            preferred_element_type=jnp.float32,
        )
        if diagonal:
            return top, total, mixed
        factor = jnp.exp2(old - top)
        return top, run_sum[turn] * factor + total, run_acc[turn] * factor + mixed

    def attend_some(first, last, k_ref, v_ref, diagonal=False):
        def step(turn, carry):
            run_max[turn], run_sum[turn], run_acc[turn] = attend(turn, k_ref, v_ref, diagonal)
            return carry

        lax.fori_loop(first, last, step, 0, unroll=min(4, last - first))

    def y_there(hop):
        return pair + side >= hop

    middle = n_head // 2
    spans = ((0, middle), (middle, n_head))

    def own_half(at):
        attend_some(*spans[at], own_k, own_v, True)

    def z_half(hop, at):
        @pl.when(pair >= hop)
        def _():
            attend_some(*spans[at], z_k.at[hop - 1], z_v.at[hop - 1])

    def y_half(hop, at):
        @pl.when(y_there(hop))
        def _():
            if at == 0:
                y_wait(hop)
            attend_some(*spans[at], y_k.at[hop - 1], y_v.at[hop - 1])

    def y_wait(hop):
        for part in range(len(parts)):
            y_copy(0, hop, part).wait_recv()

    def pass_on(hop, part):
        @pl.when(pair >= hop)
        def _():
            z_copy(hop, part).wait_recv()

        sends(hop, part, lambda copy: copy.start())

    for hop in range(1, hops + 1):
        if hop == 1:
            own_half(0)
            pass_on(1, 0)
            own_half(1)
            for part in range(1, len(parts)):
                pass_on(1, part)
        else:
            for at in range(2):
                z_half(hop - 1, at)
                pass_on(hop, at)
            y_half(hop - 1, 0)
            pass_on(hop, 2)
            if hop < hops:
                y_half(hop - 1, 1)
            pass_on(hop, 3)

    def out_copy(turn, slot):
        return pltpu.make_async_remote_copy(
            src_ref=stage.at[turn],
            dst_ref=out_ref.at[slot],
            send_sem=o_send.at[turn],
            recv_sem=o_recv.at[turn],
            device_id={"head": flip(head, n_head - 1 - turn)},
            device_id_type=MESH,
        )

    own_copy = pltpu.make_async_copy(stage.at[n_head - 1], out_ref.at[head], in_sem.at[0])
    lse_copy = pltpu.make_async_copy(lse_rows, lse_ref, in_sem.at[1])
    def finish(turn, sums):
        top, total, mixed = sums
        total = jnp.broadcast_to(
            jnp.sum(total, axis=1, keepdims=True), (groups * piece, LANES)
        )
        normed = (mixed * (1.0 / total)).astype(jnp.bfloat16)
        for group in range(groups):
            stage[turn, :, pl.ds(group * head_dim, head_dim)] = normed[
                group * piece : (group + 1) * piece
            ]
        if turn < n_head - 1:
            out_copy(turn, head).start()
        else:
            own_copy.start()
        run_max[turn] = top
        run_sum[turn] = total

    for at in range(2):
        if at == 1 and hops > 1:
            y_half(hops - 1, 1)
        z_half(hops, at)

        @pl.when(y_there(hops))
        def _():
            if at == 0:
                y_wait(hops)
            for turn in range(*spans[at]):
                finish(turn, attend(turn, y_k.at[hops - 1], y_v.at[hops - 1], False))

        @pl.when(pair + side < hops)
        def _():
            for turn in range(*spans[at]):
                finish(turn, (run_max[turn], run_sum[turn], run_acc[turn]))

    lane = lax.broadcasted_iota(jnp.int32, (piece, LANES), 1)
    for turn in range(n_head):
        dest = flip(head, n_head - 1 - turn)
        log_sum = run_max[turn] * math.log(2.0) + jnp.log(run_sum[turn])
        columns = jnp.zeros((piece, LANES), jnp.float32)
        for group in range(groups):
            columns = jnp.where(
                lane == group, log_sum[group * piece : (group + 1) * piece], columns
            )
        lse_cols[pl.ds(pl.multiple_of(dest * piece, piece), piece), :] = columns

    lse_rows[...] = jnp.transpose(lse_cols[...])[:groups]
    lse_copy.start()

    own_copy.wait()
    lse_copy.wait()
    for held in range(hops + 1):
        for part in range(len(parts)):
            sends(held, part, lambda copy: copy.wait_send())
    for turn in range(n_head - 1):
        out_copy(turn, head).wait_send()
    for turn in range(n_head - 1):
        out_copy(turn, flip(head, n_head - 1 - turn)).wait_recv()


def hand_over(out_from, lse_from, out_to, lse_to, out_held, lse_held, in_sem, out_sem):
    count = out_from.shape[0]
    froms = [out_from.at[at] for at in range(count)] + [lse_from]
    helds = [out_held.at[at] for at in range(count)] + [lse_held]
    tos = [out_to.at[at] for at in range(count)] + [lse_to.at[0]]
    ins = [
        pltpu.make_async_copy(froms[at], helds[at], in_sem.at[at]) for at in range(count + 1)
    ]
    outs = [
        pltpu.make_async_copy(helds[at], tos[at], out_sem.at[at]) for at in range(count + 1)
    ]
    for copy in ins:
        copy.start()
    for at in range(count + 1):
        ins[at].wait()
        outs[at].start()
    for copy in outs:
        copy.wait()


def body(n_ctx, n_head, queries, keys, values, documents):
    span, width = queries.shape[1:]
    head_dim = keys.shape[2]
    groups = width // head_dim
    piece, hops, tail = span // n_head, n_ctx // 4, 16
    hbm = pl.BlockSpec(memory_space=pltpu.HBM)
    bf16, f32 = jnp.bfloat16, jnp.float32
    stacked = (n_head, groups * piece, LANES)
    out, lse = pl.pallas_call(
        functools.partial(kernel, n_ctx, n_head),
        out_shape=(
            jax.ShapeDtypeStruct((n_head, piece, width), bf16),
            jax.ShapeDtypeStruct((groups, span), f32),
        ),
        in_specs=[hbm] * 4,
        out_specs=(hbm, hbm),
        scratch_shapes=[
            pltpu.VMEM((1, span), jnp.int32),
            pltpu.VMEM((span, width), bf16),
            pltpu.VMEM((n_head, groups * piece, head_dim), bf16),
            pltpu.VMEM((n_head, piece, LANES), f32),
            pltpu.VMEM((n_head, piece, LANES), jnp.int32),
            pltpu.VMEM((span + tail, head_dim), bf16),
            pltpu.VMEM((span, head_dim), bf16),
            pltpu.VMEM((hops, span + tail, head_dim), bf16),
            pltpu.VMEM((hops, span, head_dim), bf16),
            pltpu.VMEM((hops, span + tail, head_dim), bf16),
            pltpu.VMEM((hops, span, head_dim), bf16),
            pltpu.VMEM(stacked, f32),
            pltpu.VMEM(stacked, f32),
            pltpu.VMEM(stacked, f32),
            pltpu.VMEM((n_head, piece, width), bf16),
            pltpu.VMEM((span, LANES), f32),
            pltpu.VMEM((groups, span), f32),
            pltpu.SemaphoreType.DMA((4,)),
            pltpu.SemaphoreType.DMA((hops, 4)),
            pltpu.SemaphoreType.DMA((hops, 4)),
            pltpu.SemaphoreType.DMA((hops, 4)),
            pltpu.SemaphoreType.DMA((hops, 4)),
            pltpu.SemaphoreType.DMA((n_head,)),
            pltpu.SemaphoreType.DMA((n_head,)),
        ],
        compiler_params=pltpu.CompilerParams(
            collective_id=0, has_side_effects=True, vmem_limit_bytes=VMEM_GRANT
        ),
        cost_estimate=pl.CostEstimate(
            flops=2 * 2 * span * width * span * (2 * hops + 1),
            bytes_accessed=4 * span * width,
            transcendentals=span * groups * span * (2 * hops + 1),
        ),
    )(queries[0], keys[0], values[0], documents)
    out, lse = pl.pallas_call(
        hand_over,
        out_shape=(
            jax.ShapeDtypeStruct((n_head, piece, width), bf16),
            jax.ShapeDtypeStruct((1, groups, span), f32),
        ),
        in_specs=[hbm, hbm],
        out_specs=(hbm, hbm),
        scratch_shapes=[
            pltpu.VMEM((n_head, piece, width), bf16),
            pltpu.VMEM((groups, span), f32),
            pltpu.SemaphoreType.DMA((n_head + 1,)),
            pltpu.SemaphoreType.DMA((n_head + 1,)),
        ],
        compiler_params=pltpu.CompilerParams(vmem_limit_bytes=VMEM_GRANT),
    )(out, lse)
    return out, lse


def solution(mesh):
    n_ctx, n_head = mesh.shape["ctx"], mesh.shape["head"]
    in_specs = (
        P("head", "ctx", None),
        P("head", "ctx", None),
        P("head", "ctx", None),
        P("head", "ctx"),
    )
    out_specs = (P(None, ("ctx", "head"), None), P("head", None, "ctx"))
    return jax.shard_map(
        functools.partial(body, n_ctx, n_head),
        mesh=mesh,
        in_specs=in_specs,
        out_specs=out_specs,
        check_vma=False,
    )
```
